128 devices in a mesh: role: 2 (over core), dev: 64 (over x, z, y).
Axes of the slice: x: 4, y: 4, z: 4, core: 2. Of those that a mesh axis runs over, the one named last changes fastest.
Arguments:
- table_rows: bfloat16 [128, 2048, 128], P('dev'), may hold values from -6 to 6
- piece_table: int32 [128], replicated, may hold values from 0 to 25, as said below
- bag_rows: int32 [128, 32768], P('dev'), may hold values from 0 to 2047
- bag_of: int32 [128, 32768], P('dev'), may hold values from 0 to 16383, never falling along the last dimension, each value on 1 to 8 neighbouring positions
- bag_weight: bfloat16 [128, 32768], P('dev'), may hold values from 0.25 to 2
- dense_input: bfloat16 [16384, 128], P('dev'), may hold values from -6 to 6
- labels: float32 [16384], P('dev'), may hold values from 0 to 1
- cross_u: bfloat16 [3456, 512], replicated, may hold values from -0.109375 to 0.109375
- cross_v: bfloat16 [512, 3456], replicated, may hold values from -0.25 to 0.25
- cross_bias: float32 [3456], replicated, may hold values from -3 to 3
- top_w1: bfloat16 [3456, 1024], replicated, may hold values from -0.109375 to 0.109375
- top_b1: float32 [1024], replicated, may hold values from -3 to 3
- out_w: bfloat16 [1024], replicated, may hold values from -0.375 to 0.375
Outputs:
- piece_grads: bfloat16 [64, 256, 128, 128], P(None, 'role', 'dev')
The draws below stay inside these ranges and needn't reach their ends.
Inputs may be any that keep to these rules, and one draw needn't show every extreme that they name: `piece_table`: every one of the 26 tables owns one piece or more. `bag_of`: in each piece the bag numbers never fall along the lookups, and every sample has 1 to 8 lookups in every piece.
All inputs are finite; a program needn't handle non-finite values.
Results may differ from the reference program's by a relative error of at most 0.012.
The reference program's roundings to bfloat16 on the way count: a program that leaves them out, or rounds other values in their place, can miss the bound.
Values may be sent and summed in bfloat16 or wider, within the bound.
No kernel may reach another device: no remote copies, remote signals or barrier semaphores. Data moves between devices by JAX's collectives and lax.ppermute only.
A program may use at most 128 MiB of HBM per device.

```python
import math
import jax
import jax.numpy as jnp
import numpy as np
from jax import lax

E = 128
TABLES = 26
RANK = 512
HIDDEN_SIZE = 1024
TOK_DEV = 256
ROWS_PIECE = 2048
MOST = 8
PIECES = 128
BATCH = 16384
LOOKS_PIECE = 32768
WIDTH = 3456
N_DEV = 64


def placement_helper(key):
    key_first = jax.random.fold_in(key, 11)
    key_second = jax.random.fold_in(key, 12)
    key_third = jax.random.fold_in(key, 13)
    leading = jax.random.permutation(key_first, TABLES).astype(jnp.int32)
    surplus = jax.random.randint(key_second, (PIECES - TABLES,), 0, TABLES).astype(jnp.int32)
    assigned = jnp.concatenate([leading, surplus])
    shuffle = jax.random.permutation(key_third, PIECES)
    return assigned[shuffle].astype(jnp.int32)


def draw_piece_table(key, part):
    return placement_helper(key)


def set_ends(values, key, least, top_value):
    dims = values.shape
    spot = [jax.random.randint(jax.random.fold_in(key, axis), (), 0, dims[axis]) for axis in range(len(dims))]
    values = values.at[tuple(spot)].set(least)
    longest = dims.index(max(dims))
    spot[longest] = (spot[longest] + 1) % dims[longest]
    return values.at[tuple(spot)].set(top_value)


def shard_levels(own_key, shape, cuts, smallest, high):
    gain = 1.0
    for axis_at, parts in cuts:
        heights = jax.random.uniform(jax.random.fold_in(jax.random.fold_in(own_key, 6), axis_at), (parts,), jnp.float32, smallest / len(cuts), high / len(cuts))
        gain = gain * jnp.repeat(jnp.exp(heights), shape[axis_at] // parts).reshape((-1,) + (1,) * (len(shape) - 1 - axis_at))
    return gain


def length_profile(amount, total, limit, skew):
    weights = [(1 << 20) // math.isqrt(grade ** skew) + 1 for grade in range(2, amount + 1)]
    rest, given = total - limit - (amount - 1), [1] * (amount - 1)
    while rest > 0:
        free = [i for i in range(amount - 1) if given[i] < limit]
        pool, budget = sum([weights[i] for i in free]), rest
        for i in free:
            extra = min(limit - given[i], max(1, budget * weights[i] // pool), rest)
            given[i] = given[i] + extra
            rest = rest - extra
    return np.array([limit] + given)


def ragged_sizes(stream_key, amount, total, most, lean):
    if amount == 2:
        one = jax.random.randint(stream_key, (), max(1, total - most), min(most, total - 1) + 1)
        return jnp.stack([one, total - one])
    lengths = jnp.asarray(length_profile(amount, total, most, lean), jnp.int32)
    pairs = (amount - 1) // 2
    donor, sink = lengths[1:1 + 2 * pairs:2], lengths[2:2 + 2 * pairs:2]
    margin = jnp.minimum(donor - 1, most - sink)
    passed = jax.random.randint(jax.random.fold_in(stream_key, 1), (pairs,), 0, 1 << 20) % (margin + 1)
    lengths = lengths.at[1:1 + 2 * pairs:2].set(donor - passed).at[2:2 + 2 * pairs:2].set(sink + passed)
    return lengths[jax.random.permutation(jax.random.fold_in(stream_key, 2), amount)]


def normal_values(key, shape, width, reach, split=(), dtype=jnp.bfloat16):
    entries = jax.random.normal(key, shape, jnp.float32) * width
    if len(split) > 0:
        entries = shard_levels(key, shape, split, -0.22, 0.18) * entries
    return jnp.clip(entries, min=-reach, max=reach).astype(dtype)


def setup_inputs(seed: int = 0) -> dict:
    key_list = jax.random.split(jax.random.key(seed), 14)
    return {
        "table_rows": normal_values(key_list[0], (PIECES, ROWS_PIECE, E), 1.0, 6.0, ((0, 64),)),
        "piece_table": draw_piece_table(jax.random.fold_in(key_list[13], 71), 0),
        "bag_rows": set_ends(jax.random.randint(key_list[2], (PIECES, LOOKS_PIECE), 0, ROWS_PIECE), jax.random.fold_in(key_list[2], 1), 0, ROWS_PIECE - 1).astype(jnp.int32),
        "bag_of": jax.vmap(lambda own: jnp.searchsorted(jnp.cumsum(ragged_sizes(own, BATCH, LOOKS_PIECE, MOST, 2)), jnp.arange(LOOKS_PIECE), side="right"))(jax.random.split(key_list[3], PIECES)).reshape((PIECES, LOOKS_PIECE)).astype(jnp.int32),
        "bag_weight": jnp.clip(jnp.exp(math.log(2.0) - 2.0794415 * jax.random.uniform(key_list[4], (PIECES, LOOKS_PIECE), jnp.float32) ** shard_levels(key_list[4], (PIECES, LOOKS_PIECE), ((0, 64),), -0.2, 0.2)), 0.25, 2.0).astype(jnp.bfloat16),
        "dense_input": normal_values(key_list[5], (BATCH, E), 1.0, 6.0, ((0, 64),)),
        "labels": jnp.clip(1.0 * jax.random.uniform(key_list[6], (BATCH,), jnp.float32) ** shard_levels(key_list[6], (BATCH,), ((0, 64),), -0.2, 0.2), 0.0, 1.0),
        "cross_u": normal_values(key_list[7], (WIDTH, RANK), WIDTH ** -0.5, 0.109375),
        "cross_v": normal_values(key_list[8], (RANK, WIDTH), RANK ** -0.5, 0.25),
        "cross_bias": normal_values(key_list[9], (WIDTH,), 0.5, 3.0, (), jnp.float32),
        "top_w1": normal_values(key_list[10], (WIDTH, HIDDEN_SIZE), WIDTH ** -0.5, 0.109375),
        "top_b1": normal_values(key_list[11], (HIDDEN_SIZE,), 0.5, 3.0, (), jnp.float32),
        "out_w": normal_values(key_list[12], (HIDDEN_SIZE,), (HIDDEN_SIZE // 4) ** -0.5, 0.375),
    }


def dense_grads(pooled, dense_in, label_rows, cross_u, cross_v, cross_bias, top_w1, top_b1, out_w):
    row_count = pooled.shape[0]
    embed_width = dense_in.shape[1]
    features = jnp.concatenate([dense_in.astype(jnp.float32)[:, None, :], pooled], axis=1).reshape(row_count, -1)
    low_rank = jnp.dot(features.astype(jnp.bfloat16), cross_u, preferred_element_type=jnp.float32).astype(jnp.bfloat16)
    cross_out = jnp.dot(low_rank, cross_v, preferred_element_type=jnp.float32) + cross_bias
    mixed = (features * cross_out + features).astype(jnp.bfloat16)
    pre_act = jnp.dot(mixed, top_w1, preferred_element_type=jnp.float32) + top_b1
    out_weight = out_w.astype(jnp.float32)
    sig_act = jax.nn.sigmoid(pre_act)
    logits = jnp.sum(pre_act * sig_act * out_weight, axis=1)
    grad_logit = jax.nn.sigmoid(logits) - label_rows
    slope = sig_act * (1.0 + pre_act * (1.0 - sig_act))
    grad_act = (grad_logit[:, None] * out_weight * slope).astype(jnp.bfloat16)
    grad_mixed = jnp.dot(grad_act, top_w1.T, preferred_element_type=jnp.float32)
    grad_cross = (grad_mixed * features).astype(jnp.bfloat16)
    grad_low = jnp.dot(grad_cross, cross_v.T, preferred_element_type=jnp.float32).astype(jnp.bfloat16)
    grad_features = grad_mixed * (cross_out + 1.0) + jnp.dot(grad_low, cross_u.T, preferred_element_type=jnp.float32)
    return grad_features.reshape(row_count, -1, embed_width)[:, 1:, :].astype(jnp.bfloat16)


def reference(table_rows, piece_table, bag_rows, bag_of, bag_weight, dense_input, labels, cross_u, cross_v, cross_bias, top_w1, top_b1, out_w):
    def add_piece(pooled, element):
        piece_rows, table_id, row_ids, bag_ids, weights = element
        picked = piece_rows[row_ids].astype(jnp.float32)
        summed = jax.ops.segment_sum(picked * weights.astype(jnp.float32)[:, None], bag_ids, num_segments=BATCH)
        rounded = lax.optimization_barrier(summed.astype(jnp.bfloat16)).astype(jnp.float32)
        current = lax.dynamic_index_in_dim(pooled, table_id, 1, keepdims=False)
        return lax.dynamic_update_index_in_dim(pooled, current + rounded, table_id, 1), None

    pooled, _ = lax.scan(add_piece, jnp.zeros((BATCH, TABLES, E), jnp.float32), (table_rows, piece_table, bag_rows, bag_of, bag_weight))
    grad_pooled = dense_grads(pooled, dense_input, labels, cross_u, cross_v, cross_bias, top_w1, top_b1, out_w)
    selected = jnp.take(grad_pooled, piece_table, axis=1)
    return selected.reshape(N_DEV, TOK_DEV, PIECES, E)
```

```python
import functools

import jax
import jax.numpy as jnp
from jax import lax
from jax.experimental import pallas as pl
from jax.experimental.pallas import tpu as pltpu
from jax.sharding import PartitionSpec as P

LANES = 128
CHUNK = 256
WINDOW = 272
FOLD = 512
INNER = 8
MIB = 2**20


def pool_kernel(
    role_ref, first_ref, table_ref, rows_ref, bag_ref, weight_ref, out_ref, folded, pooled, prev, sem
):
    step = pl.program_id(0)
    role = role_ref[0]
    groups = table_ref.shape[1] // FOLD

    @pl.when(step == 0)
    def _():
        for group in range(groups):
            folded[:, group * LANES : (group + 1) * LANES] = table_ref[
                0, group * FOLD : (group + 1) * FOLD, :
            ]
        prev[...] = jnp.zeros_like(prev)

    top = role == 0
    rows = rows_ref[...]
    rows = jnp.where(top, rows[0:1], rows[1:2])
    bags = bag_ref[...]
    bags = jnp.where(top, bags[0:1], bags[1:2])
    weights = weight_ref[...].astype(jnp.float32)
    weights = jnp.where(top, weights[0:1], weights[1:2])
    for inner in range(INNER):
        chunk = step * INNER + inner
        lo = inner * CHUNK
        turned = [
            jnp.broadcast_to(rows[:, at : at + LANES], (LANES, LANES)).T
            for at in range(lo, lo + CHUNK, LANES)
        ]
        index = jnp.concatenate(turned, axis=0)
        within = index & (FOLD - 1)
        group_of = index // FOLD
        lane = lax.broadcasted_iota(jnp.int32, (CHUNK, LANES), 1)
        hot = jnp.concatenate(
            [
                jnp.where(within == lane + at, 1.0, 0.0).astype(jnp.bfloat16)
                for at in range(0, FOLD, LANES)
            ],
            axis=1,
        )
        wide = jnp.dot(hot, folded[...], preferred_element_type=jnp.float32)
        picked = wide[:, :LANES]
        for group in range(1, groups):
            picked = jnp.where(
                group_of == group, wide[:, group * LANES : (group + 1) * LANES], picked
            )
        picked = picked.astype(jnp.bfloat16)
        base = pl.multiple_of(first_ref[role, chunk] // 16 * 16, 16)
        before = first_ref[role, jnp.maximum(chunk - 1, 0)] // 16 * 16
        shift = pl.multiple_of(base - before, 16)
        slot = bags[:, lo : lo + CHUNK] - base
        sub = lax.broadcasted_iota(jnp.int32, (WINDOW, CHUNK), 0)
        spread = jnp.where(sub == slot, weights[:, lo : lo + CHUNK], 0.0).astype(jnp.bfloat16)
        sums = jnp.dot(spread, picked, preferred_element_type=jnp.float32)
        head = sums[:16] + prev[pl.ds(shift, 16), :]
        prev[:16, :] = head
        prev[16:, :] = sums[16:]
        pooled[pl.ds(base, 16), :] = head.astype(jnp.bfloat16)
        pooled[pl.ds(pl.multiple_of(base + 16, 16), WINDOW - 16), :] = sums[16:].astype(
            jnp.bfloat16
        )

    @pl.when(step == pl.num_programs(0) - 1)
    def _():
        copy = pltpu.make_async_copy(pooled.at[pl.ds(0, out_ref.shape[0])], out_ref, sem)
        copy.start()
        copy.wait()


def pool_piece(role, table_rows, bag_rows, bag_of, bag_weight, bag_count):
    looks = bag_rows.shape[1]
    length, width = table_rows.shape[1:]
    block = CHUNK * INNER
    firsts = bag_of.reshape(bag_of.shape[0], -1, CHUNK)[:, :, 0]
    return pl.pallas_call(
        pool_kernel,
        grid_spec=pltpu.PrefetchScalarGridSpec(
            num_scalar_prefetch=2,
            grid=(looks // block,),
            in_specs=[
                pl.BlockSpec((1, length, width), lambda i, role, firsts: (role[0], 0, 0)),
                pl.BlockSpec((2, block), lambda i, role, firsts: (0, i)),
                pl.BlockSpec((2, block), lambda i, role, firsts: (0, i)),
                pl.BlockSpec((2, block), lambda i, role, firsts: (0, i)),
            ],
            out_specs=pl.BlockSpec(memory_space=pl.ANY),
            scratch_shapes=[
                pltpu.VMEM((FOLD, length // FOLD * width), jnp.bfloat16),
                pltpu.VMEM((bag_count + WINDOW, width), jnp.bfloat16),
                pltpu.VMEM((WINDOW, width), jnp.float32),
                pltpu.SemaphoreType.DMA,
            ],
        ),
        out_shape=jax.ShapeDtypeStruct((bag_count, width), jnp.bfloat16),
        compiler_params=pltpu.CompilerParams(vmem_limit_bytes=24 * MIB),
    )(role, firsts, table_rows, bag_rows, bag_of, bag_weight)


def against(left, right):
    return lax.dot_general(
        left, right, (((1,), (1,)), ((), ())), preferred_element_type=jnp.float32
    )


def dense_kernel(
    role_ref,
    piece_table,
    arrived,
    dense_ref,
    label_ref,
    cross_u,
    cross_v,
    bias_ref,
    top_w1,
    top_b1,
    out_w,
    out_ref,
    landed,
    features,
    cross,
    mixed,
    grad_mixed,
    grads,
    woven,
    sems,
):
    role = role_ref[0]
    pieces, rows, width = arrived.shape
    columns = features.shape[1]
    parts = sems.shape[0]
    per_part = pieces // parts

    def part_copy(part):
        span = pl.ds(part * per_part, per_part)
        return pltpu.make_async_copy(arrived.at[span], landed.at[span], sems.at[part])

    for part in range(parts):
        part_copy(part).start()
    features[...] = jnp.zeros_like(features)
    features[:, :width] = dense_ref[pl.ds(pl.multiple_of(role * rows, 16), rows), :].astype(
        jnp.float32
    )
    for part in range(parts):
        part_copy(part).wait()

        @pl.loop(part * per_part, (part + 1) * per_part, unroll=4)
        def _(piece):
            place = pl.multiple_of((piece_table[piece] + 1) * width, width)
            features[:, pl.ds(place, width)] += landed[piece].astype(jnp.float32)

    blocks = [(at, min(256, columns - at)) for at in range(0, columns, 256)]
    low_rank = jnp.dot(
        features[...].astype(jnp.bfloat16), cross_u[...], preferred_element_type=jnp.float32
    ).astype(jnp.bfloat16)
    for at, size in blocks:
        span = pl.ds(at, size)
        part_cross = (
            jnp.dot(low_rank, cross_v[:, span], preferred_element_type=jnp.float32)
            + bias_ref[:, span]
        )
        cross[:, span] = part_cross
        part_features = features[:, span]
        mixed[:, span] = (part_features * part_cross + part_features).astype(jnp.bfloat16)
    pre_act = jnp.dot(mixed[...], top_w1[...], preferred_element_type=jnp.float32) + top_b1[...]
    out_weight = out_w[...].astype(jnp.float32)
    sig_act = jax.nn.sigmoid(pre_act)
    logits = jnp.sum(pre_act * sig_act * out_weight, axis=1, keepdims=True)
    label_row = jnp.where(role == 0, label_ref[0:1, :], label_ref[1:2, :])
    label_column = jnp.broadcast_to(label_row, (rows, rows)).T[:, 0:1]
    grad_logit = jax.nn.sigmoid(logits) - label_column
    slope = sig_act * (1.0 + pre_act * (1.0 - sig_act))
    grad_act = (grad_logit * out_weight * slope).astype(jnp.bfloat16)
    for at, size in blocks:
        span = pl.ds(at, size)
        part_grad = against(grad_act, top_w1[span, :])
        grad_mixed[:, span] = part_grad
        mixed[:, span] = (part_grad * features[:, span]).astype(jnp.bfloat16)
    grad_low = against(mixed[...], cross_v[...]).astype(jnp.bfloat16)
    for at, size in blocks:
        span = pl.ds(at, size)
        total = grad_mixed[:, span] * (cross[:, span] + 1.0) + against(grad_low, cross_u[span, :])
        for inner in range(0, size, width):
            slot = (at + inner) // width - 1
            if slot >= 0:
                grads[slot] = total[:, inner : inner + width]

    @pl.loop(0, pieces // 2, unroll=4)
    def _(dest):
        slot = lax.rem(dest, woven.shape[0])
        for side in range(2):
            woven[slot, pl.ds(side, rows, stride=2), :] = grads[piece_table[2 * dest + side]]
        out_ref[dest] = woven[slot].astype(jnp.bfloat16)


def dense_side(
    role, piece_table, arrived, dense_input, labels, cross_u, cross_v, cross_bias, top_w1, top_b1, out_w
):
    pieces, rows, width = arrived.shape
    columns = cross_bias.shape[0]
    whole = pl.BlockSpec(memory_space=pltpu.VMEM)
    return pl.pallas_call(
        dense_kernel,
        in_specs=[
            pl.BlockSpec(memory_space=pltpu.SMEM),
            pl.BlockSpec(memory_space=pltpu.SMEM),
            pl.BlockSpec(memory_space=pl.ANY),
        ]
        + [whole] * 8,
        out_specs=whole,
        out_shape=jax.ShapeDtypeStruct((pieces // 2, 2 * rows, width), jnp.bfloat16),
        scratch_shapes=[
            pltpu.VMEM(arrived.shape, jnp.bfloat16),
            pltpu.VMEM((rows, columns), jnp.float32),
            pltpu.VMEM((rows, columns), jnp.float32),
            pltpu.VMEM((rows, columns), jnp.bfloat16),
            pltpu.VMEM((rows, columns), jnp.float32),
            pltpu.VMEM((columns // width - 1, rows, width), jnp.float32),
            pltpu.VMEM((4, 2 * rows, width), jnp.float32),
            pltpu.SemaphoreType.DMA((8,)),
        ],
        compiler_params=pltpu.CompilerParams(vmem_limit_bytes=48 * MIB),
    )(
        role,
        piece_table,
        arrived,
        dense_input,
        labels.reshape(2, rows),
        cross_u,
        cross_v,
        cross_bias.reshape(1, columns),
        top_w1,
        top_b1.reshape(1, -1),
        out_w.reshape(1, -1),
    )


def local(
    table_rows,
    piece_table,
    bag_rows,
    bag_of,
    bag_weight,
    dense_input,
    labels,
    cross_u,
    cross_v,
    cross_bias,
    top_w1,
    top_b1,
    out_w,
):
    devices = lax.axis_size("dev")
    role = lax.axis_index("role").reshape(1)
    half_rows = dense_input.shape[0] // 2
    width = dense_input.shape[1]
    pooled = pool_piece(
        role, table_rows, bag_rows, bag_of, bag_weight, devices * dense_input.shape[0]
    )
    arrived = lax.all_to_all(
        pooled.reshape(2 * devices, half_rows, width),
        ("dev", "role"),
        split_axis=0,
        concat_axis=0,
        tiled=True,
    )
    gradients = dense_side(
        role,
        piece_table,
        arrived,
        dense_input,
        labels,
        cross_u,
        cross_v,
        cross_bias,
        top_w1,
        top_b1,
        out_w,
    )
    returned = lax.all_to_all(gradients, "dev", split_axis=0, concat_axis=0, tiled=True)
    return returned.reshape(devices, half_rows, 2, width)


def solution(mesh):
    return jax.shard_map(
        local,
        mesh=mesh,
        in_specs=(
            P("dev", None, None),
            P(),
            P("dev", None),
            P("dev", None),
            P("dev", None),
            P("dev", None),
            P("dev"),
            P(),
            P(),
            P(),
            P(),
            P(),
            P(),
        ),
        out_specs=P(None, "role", "dev", None),
        check_vma=False,
    )
```

```python
import functools

import jax
import jax.numpy as jnp
from jax import lax
from jax.experimental import pallas as pl
from jax.experimental.pallas import tpu as pltpu
from jax.sharding import PartitionSpec as P

LANES = 128
CHUNK = 256
WIDEST = 272
NARROW = 192
FOLD = 512
GROUP = 4
PARTS = 8
PART = 512
MIB = 2**20


def pool_kernel(
    role_ref,
    tables,
    rows_hbm,
    bags_hbm,
    weights_hbm,
    out_hbm,
    folded,
    rows_ref,
    bags_ref,
    weights_ref,
    carried,
    picked,
    pooled,
    sems,
    out_sem,
):
    role = role_ref[0]
    folds = tables.shape[1] // FOLD
    bag_count = out_hbm.shape[0]
    span = CHUNK * GROUP
    steps = rows_ref.shape[1] // span
    copies = [
        pltpu.make_async_copy(
            tables.at[role, pl.ds(fold * FOLD, FOLD)],
            folded.at[:, pl.ds(fold * LANES, LANES)],
            sems.at[fold],
        )
        for fold in range(folds)
    ]
    copies.append(pltpu.make_async_copy(rows_hbm, rows_ref, sems.at[folds]))
    later = [
        pltpu.make_async_copy(bags_hbm, bags_ref, sems.at[folds + 1]),
        pltpu.make_async_copy(weights_hbm, weights_ref, sems.at[folds + 2]),
    ]
    for copy in copies + later:
        copy.start()
    carried[...] = jnp.zeros_like(carried)
    for copy in copies:
        copy.wait()

    def own_row(ref, start, size):
        both = ref[:, pl.ds(pl.multiple_of(start, LANES), size)]
        if both.dtype != jnp.int32:
            both = both.astype(jnp.float32)
        return jnp.where(role == 0, both[0:1], both[1:2])

    def gather(step, slot):
        rows = own_row(rows_ref, step * span, span)
        index = jnp.concatenate(
            [
                jnp.broadcast_to(rows[:, at : at + LANES], (LANES, LANES)).T
                for at in range(0, span, LANES)
            ],
            axis=0,
        )
        within = index & (FOLD - 1)
        fold_of = index // FOLD
        lane = lax.broadcasted_iota(jnp.int32, (span, LANES), 1)
        hot = jnp.concatenate(
            [
                jnp.where(within == lane + at, 1.0, 0.0).astype(jnp.bfloat16)
                for at in range(0, FOLD, LANES)
            ],
            axis=1,
        )
        wide = jnp.dot(hot, folded[...], preferred_element_type=jnp.float32)
        found = wide[:, :LANES]
        for fold in range(1, folds):
            found = jnp.where(fold_of == fold, wide[:, fold * LANES : (fold + 1) * LANES], found)
        picked[slot] = found.astype(jnp.bfloat16)

    def scatter(step, slot, window, before):
        bags = own_row(bags_ref, step * span, span)
        weights = own_row(weights_ref, step * span, span)
        for inner in range(GROUP):
            at = inner * CHUNK
            base = jnp.minimum(bags[0, at] // 16 * 16, bag_count - window)
            place = bags[:, at : at + CHUNK] - base
            sub = lax.broadcasted_iota(jnp.int32, (window, CHUNK), 0)
            spread = jnp.where(sub == place, weights[:, at : at + CHUNK], 0.0).astype(jnp.bfloat16)
            sums = jnp.dot(
                spread, picked[slot, at : at + CHUNK, :], preferred_element_type=jnp.float32
            ) + carried[pl.ds(pl.multiple_of(base - before, 16), window), :]
            carried[:window, :] = sums
            pooled[pl.ds(pl.multiple_of(base, 16), window), :] = sums.astype(jnp.bfloat16)
            before = base
        return before

    def send(begin, end):
        def one(part, carry):
            rows = pl.ds(pl.multiple_of(part * PART, PART), PART)
            pltpu.make_async_copy(pooled.at[rows], out_hbm.at[rows], out_sem).start()
            return carry

        lax.fori_loop(begin // PART, end // PART, one, 0)

    gather(0, 0)
    for copy in later:
        copy.wait()

    def sweep(window):
        def pair(at, start):
            gather(2 * at + 1, 1)
            before = scatter(2 * at, 0, window, start)
            gather(2 * at + 2, 0)
            before = scatter(2 * at + 1, 1, window, before)
            send(start, before)
            return before

        start = lax.fori_loop(0, steps // 2 - 1, pair, jnp.int32(0))
        gather(steps - 1, 1)
        before = scatter(steps - 2, 0, window, start)
        scatter(steps - 1, 1, window, before)
        send(start, bag_count)

    most = jnp.zeros((2, LANES), jnp.int32)
    for at in range(0, bags_ref.shape[1], CHUNK):
        ends = bags_ref[:, at + CHUNK - LANES : at + CHUNK]
        most = jnp.maximum(most, pltpu.roll(ends, 1, 1) - bags_ref[:, at : at + LANES])
    lane = lax.broadcasted_iota(jnp.int32, (2, LANES), 1)
    even = jnp.max(jnp.where(lane == 0, most, 0)) < NARROW - 16

    @pl.when(even)
    def _():
        sweep(NARROW)

    @pl.when(jnp.logical_not(even))
    def _():
        sweep(WIDEST)

    pltpu.make_async_copy(pooled, out_hbm, out_sem).wait()


def in_hbm(*values):
    return [pltpu.with_memory_space_constraint(value, pltpu.HBM) for value in values]


def pool_piece(role, table_rows, bag_rows, bag_of, bag_weight, bag_count):
    length, width = table_rows.shape[1:]
    anywhere = pl.BlockSpec(memory_space=pl.ANY)
    return pl.pallas_call(
        pool_kernel,
        in_specs=[pl.BlockSpec(memory_space=pltpu.SMEM)] + [anywhere] * 4,
        out_specs=anywhere,
        out_shape=pltpu.HBM((bag_count, width), jnp.bfloat16),
        scratch_shapes=[
            pltpu.VMEM((FOLD, length // FOLD * width), jnp.bfloat16),
            pltpu.VMEM(bag_rows.shape, jnp.int32),
            pltpu.VMEM(bag_of.shape, jnp.int32),
            pltpu.VMEM(bag_weight.shape, jnp.bfloat16),
            pltpu.VMEM((2 * WIDEST, width), jnp.float32),
            pltpu.VMEM((2, CHUNK * GROUP, width), jnp.bfloat16),
            pltpu.VMEM((bag_count, width), jnp.bfloat16),
            pltpu.SemaphoreType.DMA((length // FOLD + 3,)),
            pltpu.SemaphoreType.DMA,
        ],
        compiler_params=pltpu.CompilerParams(vmem_limit_bytes=56 * MIB),
    )(role, *in_hbm(table_rows, bag_rows, bag_of, bag_weight))


def against(left, right):
    return lax.dot_general(
        left, right, (((1,), (1,)), ((), ())), preferred_element_type=jnp.float32
    )


def dense_kernel(role_ref, *refs):
    count = 10
    given, out_hbm, held = refs[:count], refs[count], refs[count + 1 : 2 * count + 1]
    features, cross, mixed, grad_mixed, grads, woven, leaving, sems, out_sem = refs[2 * count + 1 :]
    arrived, piece_table, dense_ref, label_ref, cross_u, cross_v, bias_ref, top_w1 = held[:8]
    top_b1, out_w = held[8:]
    role = role_ref[0]
    pieces, rows, width = arrived.shape
    columns = features.shape[1]
    copies = [
        pltpu.make_async_copy(source, target, sems.at[at])
        for at, (source, target) in enumerate(zip(given[1:], held[1:]))
    ]
    parts = PARTS
    per_part = pieces // parts
    arrivals = [
        pltpu.make_async_copy(
            given[0].at[pl.ds(part * per_part, per_part)],
            arrived.at[pl.ds(part * per_part, per_part)],
            sems.at[count - 1 + part],
        )
        for part in range(parts)
    ]
    copies[0].start()
    copies[1].start()
    for copy in arrivals + copies[2:]:
        copy.start()
    features[...] = jnp.zeros_like(features)
    copies[0].wait()
    copies[1].wait()
    features[:, :width] = dense_ref[pl.ds(pl.multiple_of(role * rows, 16), rows), :].astype(
        jnp.float32
    )
    for part in range(parts):
        arrivals[part].wait()

        @pl.loop(part * per_part, (part + 1) * per_part, unroll=4)
        def _(piece):
            place = pl.multiple_of((piece_table[0, piece] + 1) * width, width)
            features[:, pl.ds(place, width)] += arrived[piece].astype(jnp.float32)

    for copy in copies[2:]:
        if copy is not copies[6]:
            copy.wait()
    blocks = [(at, min(256, columns - at)) for at in range(0, columns, 256)]
    low_rank = jnp.dot(
        features[...].astype(jnp.bfloat16), cross_u[...], preferred_element_type=jnp.float32
    ).astype(jnp.bfloat16)
    for at, size in blocks:
        span = pl.ds(at, size)
        part_cross = (
            jnp.dot(low_rank, cross_v[:, span], preferred_element_type=jnp.float32)
            + bias_ref[:, span]
        )
        cross[:, span] = part_cross
        part_features = features[:, span]
        mixed[:, span] = (part_features * part_cross + part_features).astype(jnp.bfloat16)
    copies[6].wait()
    pre_act = jnp.dot(mixed[...], top_w1[...], preferred_element_type=jnp.float32) + top_b1[...]
    out_weight = out_w[...].astype(jnp.float32)
    sig_act = jax.nn.sigmoid(pre_act)
    logits = jnp.sum(pre_act * sig_act * out_weight, axis=1, keepdims=True)
    label_row = jnp.where(role == 0, label_ref[0:1, :], label_ref[1:2, :])
    label_column = jnp.broadcast_to(label_row, (rows, rows)).T[:, 0:1]
    grad_logit = jax.nn.sigmoid(logits) - label_column
    slope = sig_act * (1.0 + pre_act * (1.0 - sig_act))
    grad_act = (grad_logit * out_weight * slope).astype(jnp.bfloat16)
    for at, size in blocks:
        span = pl.ds(at, size)
        part_grad = against(grad_act, top_w1[span, :])
        grad_mixed[:, span] = part_grad
        mixed[:, span] = (part_grad * features[:, span]).astype(jnp.bfloat16)
    grad_low = against(mixed[...], cross_v[...]).astype(jnp.bfloat16)
    for at, size in blocks:
        span = pl.ds(at, size)
        total = grad_mixed[:, span] * (cross[:, span] + 1.0) + against(grad_low, cross_u[span, :])
        for inner in range(0, size, width):
            slot = (at + inner) // width - 1
            if slot >= 0:
                grads[slot] = total[:, inner : inner + width]

    @pl.loop(0, pieces // 2, unroll=4)
    def _(dest):
        slot = lax.rem(dest, woven.shape[0])
        for side in range(2):
            woven[slot, pl.ds(side, rows, stride=2), :] = grads[piece_table[0, 2 * dest + side]]
        leaving[dest] = woven[slot].astype(jnp.bfloat16)
        pltpu.make_async_copy(leaving.at[dest], out_hbm.at[dest], out_sem).start()

    pltpu.make_async_copy(leaving, out_hbm, out_sem).wait()


def dense_side(
    role, piece_table, arrived, dense_input, labels, cross_u, cross_v, cross_bias, top_w1, top_b1, out_w
):
    pieces, rows, width = arrived.shape
    columns = cross_bias.shape[0]
    anywhere = pl.BlockSpec(memory_space=pl.ANY)
    given = (
        arrived,
        piece_table.reshape(1, pieces),
        dense_input,
        labels.reshape(2, rows),
        cross_u,
        cross_v,
        cross_bias.reshape(1, columns),
        top_w1,
        top_b1.reshape(1, -1),
        out_w.reshape(1, -1),
    )
    held = [pltpu.VMEM(value.shape, value.dtype) for value in given]
    held[1] = pltpu.SMEM((1, pieces), jnp.int32)
    return pl.pallas_call(
        dense_kernel,
        in_specs=[pl.BlockSpec(memory_space=pltpu.SMEM)] + [anywhere] * len(given),
        out_specs=anywhere,
        out_shape=pltpu.HBM((pieces // 2, 2 * rows, width), jnp.bfloat16),
        scratch_shapes=held
        + [
            pltpu.VMEM((rows, columns), jnp.float32),
            pltpu.VMEM((rows, columns), jnp.float32),
            pltpu.VMEM((rows, columns), jnp.bfloat16),
            pltpu.VMEM((rows, columns), jnp.float32),
            pltpu.VMEM((columns // width - 1, rows, width), jnp.float32),
            pltpu.VMEM((4, 2 * rows, width), jnp.float32),
            pltpu.VMEM((pieces // 2, 2 * rows, width), jnp.bfloat16),
            pltpu.SemaphoreType.DMA((len(given) - 1 + PARTS,)),
            pltpu.SemaphoreType.DMA,
        ],
        compiler_params=pltpu.CompilerParams(vmem_limit_bytes=56 * MIB),
    )(role, *in_hbm(*given))


def local(
    table_rows,
    piece_table,
    bag_rows,
    bag_of,
    bag_weight,
    dense_input,
    labels,
    cross_u,
    cross_v,
    cross_bias,
    top_w1,
    top_b1,
    out_w,
):
    devices = lax.axis_size("dev")
    role = lax.axis_index("role").reshape(1)
    half_rows = dense_input.shape[0] // 2
    width = dense_input.shape[1]
    pooled = pool_piece(
        role, table_rows, bag_rows, bag_of, bag_weight, devices * dense_input.shape[0]
    )
    arrived = lax.all_to_all(
        pooled.reshape(2 * devices, half_rows, width),
        ("dev", "role"),
        split_axis=0,
        concat_axis=0,
        tiled=True,
    )
    gradients = dense_side(
        role,
        piece_table,
        arrived,
        dense_input,
        labels,
        cross_u,
        cross_v,
        cross_bias,
        top_w1,
        top_b1,
        out_w,
    )
    gradients = gradients.reshape(devices, half_rows, 2, width)
    return lax.all_to_all(gradients, "dev", split_axis=0, concat_axis=0, tiled=True)


def solution(mesh):
    return jax.shard_map(
        local,
        mesh=mesh,
        in_specs=(
            P("dev", None, None),
            P(),
            P("dev", None),
            P("dev", None),
            P("dev", None),
            P("dev", None),
            P("dev"),
            P(),
            P(),
            P(),
            P(),
            P(),
            P(),
        ),
        out_specs=P(None, "role", "dev", None),
        check_vma=False,
    )
```

```python
import functools

import jax
import jax.numpy as jnp
from jax import lax
from jax.experimental import pallas as pl
from jax.experimental.pallas import tpu as pltpu
from jax.sharding import PartitionSpec as P

LANES = 128
CHUNK = 256
WIDEST = 272
NARROW = 192
FOLD = 512
GROUP = 4
PARTS = 8
MIB = 2**20


def pool_kernel(
    role_ref,
    tables,
    rows_hbm,
    bags_hbm,
    weights_hbm,
    pooled,
    folded,
    rows_ref,
    bags_ref,
    weights_ref,
    carried,
    picked,
    sems,
):
    role = role_ref[0]
    folds = tables.shape[1] // FOLD
    bag_count = pooled.shape[0]
    span = CHUNK * GROUP
    steps = rows_ref.shape[1] // span
    copies = [
        pltpu.make_async_copy(
            tables.at[role, pl.ds(fold * FOLD, FOLD)],
            folded.at[:, pl.ds(fold * LANES, LANES)],
            sems.at[fold],
        )
        for fold in range(folds)
    ]
    copies.append(pltpu.make_async_copy(rows_hbm, rows_ref, sems.at[folds]))
    later = [
        pltpu.make_async_copy(bags_hbm, bags_ref, sems.at[folds + 1]),
        pltpu.make_async_copy(weights_hbm, weights_ref, sems.at[folds + 2]),
    ]
    for copy in copies + later:
        copy.start()
    carried[...] = jnp.zeros_like(carried)
    for copy in copies:
        copy.wait()

    def own_row(ref, start, size):
        both = ref[:, pl.ds(pl.multiple_of(start, LANES), size)]
        if both.dtype != jnp.int32:
            both = both.astype(jnp.float32)
        return jnp.where(role == 0, both[0:1], both[1:2])

    def gather(step, slot):
        rows = own_row(rows_ref, step * span, span)
        index = jnp.concatenate(
            [
                jnp.broadcast_to(rows[:, at : at + LANES], (LANES, LANES)).T
                for at in range(0, span, LANES)
            ],
            axis=0,
        )
        within = index & (FOLD - 1)
        fold_of = index // FOLD
        lane = lax.broadcasted_iota(jnp.int32, (span, LANES), 1)
        hot = jnp.concatenate(
            [
                jnp.where(within == lane + at, 1.0, 0.0).astype(jnp.bfloat16)
                for at in range(0, FOLD, LANES)
            ],
            axis=1,
        )
        wide = jnp.dot(hot, folded[...], preferred_element_type=jnp.float32)
        found = wide[:, :LANES]
        for fold in range(1, folds):
            found = jnp.where(fold_of == fold, wide[:, fold * LANES : (fold + 1) * LANES], found)
        picked[slot] = found.astype(jnp.bfloat16)

    def scatter(step, slot, window, before):
        bags = own_row(bags_ref, step * span, span)
        weights = own_row(weights_ref, step * span, span)
        for inner in range(GROUP):
            at = inner * CHUNK
            base = jnp.minimum(bags[0, at] // 16 * 16, bag_count - window)
            place = bags[:, at : at + CHUNK] - base
            sub = lax.broadcasted_iota(jnp.int32, (window, CHUNK), 0)
            spread = jnp.where(sub == place, weights[:, at : at + CHUNK], 0.0).astype(jnp.bfloat16)
            sums = jnp.dot(
                spread, picked[slot, at : at + CHUNK, :], preferred_element_type=jnp.float32
            ) + carried[pl.ds(pl.multiple_of(base - before, 16), window), :]
            carried[:window, :] = sums
            pooled[pl.ds(pl.multiple_of(base, 16), window), :] = sums.astype(jnp.bfloat16)
            before = base
        return before

    gather(0, 0)
    for copy in later:
        copy.wait()

    def sweep(window):
        def pair(at, start):
            gather(2 * at + 1, 1)
            before = scatter(2 * at, 0, window, start)
            gather(2 * at + 2, 0)
            before = scatter(2 * at + 1, 1, window, before)
            return before

        start = lax.fori_loop(0, steps // 2 - 1, pair, jnp.int32(0))
        gather(steps - 1, 1)
        before = scatter(steps - 2, 0, window, start)
        scatter(steps - 1, 1, window, before)

    most = jnp.zeros((2, LANES), jnp.int32)
    for at in range(0, bags_ref.shape[1], CHUNK):
        ends = bags_ref[:, at + CHUNK - LANES : at + CHUNK]
        most = jnp.maximum(most, pltpu.roll(ends, 1, 1) - bags_ref[:, at : at + LANES])
    lane = lax.broadcasted_iota(jnp.int32, (2, LANES), 1)
    even = jnp.max(jnp.where(lane == 0, most, 0)) < NARROW - 16

    @pl.when(even)
    def _():
        sweep(NARROW)

    @pl.when(jnp.logical_not(even))
    def _():
        sweep(WIDEST)


def in_hbm(*values):
    return [pltpu.with_memory_space_constraint(value, pltpu.HBM) for value in values]


def pool_piece(role, table_rows, bag_rows, bag_of, bag_weight, bag_count):
    length, width = table_rows.shape[1:]
    anywhere = pl.BlockSpec(memory_space=pl.ANY)
    return pl.pallas_call(
        pool_kernel,
        in_specs=[pl.BlockSpec(memory_space=pltpu.SMEM)] + [anywhere] * 4,
        out_specs=pl.BlockSpec(memory_space=pltpu.VMEM),
        out_shape=jax.ShapeDtypeStruct((bag_count, width), jnp.bfloat16),
        scratch_shapes=[
            pltpu.VMEM((FOLD, length // FOLD * width), jnp.bfloat16),
            pltpu.VMEM(bag_rows.shape, jnp.int32),
            pltpu.VMEM(bag_of.shape, jnp.int32),
            pltpu.VMEM(bag_weight.shape, jnp.bfloat16),
            pltpu.VMEM((2 * WIDEST, width), jnp.float32),
            pltpu.VMEM((2, CHUNK * GROUP, width), jnp.bfloat16),
            pltpu.SemaphoreType.DMA((length // FOLD + 3,)),
        ],
        compiler_params=pltpu.CompilerParams(vmem_limit_bytes=40 * MIB),
    )(role, *in_hbm(table_rows, bag_rows, bag_of, bag_weight))


def against(left, right):
    return lax.dot_general(
        left, right, (((1,), (1,)), ((), ())), preferred_element_type=jnp.float32
    )


def dense_kernel(role_ref, cross_u, cross_v, top_w1, *refs):
    count = 7
    given, out_hbm, held = refs[:count], refs[count], refs[count + 1 : 2 * count + 1]
    features, cross, mixed, grad_mixed, grads, woven, leaving, sems, out_sem = refs[2 * count + 1 :]
    arrived, piece_table, dense_ref, label_ref, bias_ref, top_b1, out_w = held
    role = role_ref[0]
    pieces, rows, width = arrived.shape
    columns = features.shape[1]
    copies = [
        pltpu.make_async_copy(source, target, sems.at[at])
        for at, (source, target) in enumerate(zip(given[1:], held[1:]))
    ]
    parts = PARTS
    per_part = pieces // parts
    arrivals = [
        pltpu.make_async_copy(
            given[0].at[pl.ds(part * per_part, per_part)],
            arrived.at[pl.ds(part * per_part, per_part)],
            sems.at[count - 1 + part],
        )
        for part in range(parts)
    ]
    copies[0].start()
    for copy in arrivals + copies[1:]:
        copy.start()
    features[...] = jnp.zeros_like(features)
    copies[0].wait()
    for part in range(parts):
        arrivals[part].wait()

        @pl.loop(part * per_part, (part + 1) * per_part, unroll=4)
        def _(piece):
            place = pl.multiple_of((piece_table[0, piece] + 1) * width, width)
            features[:, pl.ds(place, width)] += arrived[piece].astype(jnp.float32)

    copies[1].wait()
    features[:, :width] = dense_ref[pl.ds(pl.multiple_of(role * rows, 16), rows), :].astype(
        jnp.float32
    )
    blocks = [(at, min(256, columns - at)) for at in range(0, columns, 256)]
    low_rank = jnp.dot(
        features[...].astype(jnp.bfloat16), cross_u[...], preferred_element_type=jnp.float32
    ).astype(jnp.bfloat16)
    copies[3].wait()
    for at, size in blocks:
        span = pl.ds(at, size)
        part_cross = (
            jnp.dot(low_rank, cross_v[:, span], preferred_element_type=jnp.float32)
            + bias_ref[span].reshape(1, size)
        )
        cross[:, span] = part_cross
        part_features = features[:, span]
        mixed[:, span] = (part_features * part_cross + part_features).astype(jnp.bfloat16)
    for at in (2, 4, 5):
        copies[at].wait()
    pre_act = jnp.dot(mixed[...], top_w1[...], preferred_element_type=jnp.float32) + top_b1[...].reshape(1, -1)
    out_weight = out_w[...].astype(jnp.float32).reshape(1, -1)
    sig_act = jax.nn.sigmoid(pre_act)
    logits = jnp.sum(pre_act * sig_act * out_weight, axis=1, keepdims=True)
    label_row = jnp.where(role == 0, label_ref[0:1, :], label_ref[1:2, :])
    label_column = jnp.broadcast_to(label_row, (rows, rows)).T[:, 0:1]
    grad_logit = jax.nn.sigmoid(logits) - label_column
    slope = sig_act * (1.0 + pre_act * (1.0 - sig_act))
    grad_act = (grad_logit * out_weight * slope).astype(jnp.bfloat16)
    for at, size in blocks:
        span = pl.ds(at, size)
        part_grad = against(grad_act, top_w1[span, :])
        grad_mixed[:, span] = part_grad
        mixed[:, span] = (part_grad * features[:, span]).astype(jnp.bfloat16)
    grad_low = against(mixed[...], cross_v[...]).astype(jnp.bfloat16)
    for at, size in blocks:
        span = pl.ds(at, size)
        total = grad_mixed[:, span] * (cross[:, span] + 1.0) + against(grad_low, cross_u[span, :])
        for inner in range(0, size, width):
            slot = (at + inner) // width - 1
            if slot >= 0:
                grads[slot] = total[:, inner : inner + width]

    @pl.loop(0, pieces // 2, unroll=4)
    def _(dest):
        slot = lax.rem(dest, woven.shape[0])
        for side in range(2):
            woven[slot, pl.ds(side, rows, stride=2), :] = grads[piece_table[0, 2 * dest + side]]
        leaving[dest] = woven[slot].astype(jnp.bfloat16)
        pltpu.make_async_copy(leaving.at[dest], out_hbm.at[dest], out_sem).start()

    pltpu.make_async_copy(leaving, out_hbm, out_sem).wait()


def dense_side(
    role, piece_table, arrived, dense_input, labels, cross_u, cross_v, cross_bias, top_w1, top_b1, out_w
):
    pieces, rows, width = arrived.shape
    columns = cross_bias.shape[0]
    anywhere = pl.BlockSpec(memory_space=pl.ANY)
    given = (
        arrived,
        piece_table.reshape(1, pieces),
        dense_input,
        labels.reshape(2, rows),
        cross_bias,
        top_b1,
        out_w,
    )
    held = [pltpu.VMEM(value.shape, value.dtype) for value in given]
    held[1] = pltpu.SMEM((1, pieces), jnp.int32)
    return pl.pallas_call(
        dense_kernel,
        in_specs=[pl.BlockSpec(memory_space=pltpu.SMEM)]
        + [pl.BlockSpec(memory_space=pltpu.VMEM)] * 3
        + [anywhere] * len(given),
        out_specs=anywhere,
        out_shape=pltpu.HBM((pieces // 2, 2 * rows, width), jnp.bfloat16),
        scratch_shapes=held
        + [
            pltpu.VMEM((rows, columns), jnp.float32),
            pltpu.VMEM((rows, columns), jnp.float32),
            pltpu.VMEM((rows, columns), jnp.bfloat16),
            pltpu.VMEM((rows, columns), jnp.float32),
            pltpu.VMEM((columns // width - 1, rows, width), jnp.float32),
            pltpu.VMEM((4, 2 * rows, width), jnp.float32),
            pltpu.VMEM((pieces // 2, 2 * rows, width), jnp.bfloat16),
            pltpu.SemaphoreType.DMA((len(given) - 1 + PARTS,)),
            pltpu.SemaphoreType.DMA,
        ],
        compiler_params=pltpu.CompilerParams(vmem_limit_bytes=40 * MIB),
    )(role, cross_u, cross_v, top_w1, *in_hbm(*given))


def local(
    table_rows,
    piece_table,
    bag_rows,
    bag_of,
    bag_weight,
    dense_input,
    labels,
    cross_u,
    cross_v,
    cross_bias,
    top_w1,
    top_b1,
    out_w,
):
    devices = lax.axis_size("dev")
    role = lax.axis_index("role").reshape(1)
    half_rows = dense_input.shape[0] // 2
    width = dense_input.shape[1]
    pooled = pool_piece(
        role, table_rows, bag_rows, bag_of, bag_weight, devices * dense_input.shape[0]
    )
    arrived = lax.all_to_all(
        pooled.reshape(2 * devices, half_rows, width),
        ("dev", "role"),
        split_axis=0,
        concat_axis=0,
        tiled=True,
    )
    gradients = dense_side(
        role,
        piece_table,
        arrived,
        dense_input,
        labels,
        cross_u,
        cross_v,
        cross_bias,
        top_w1,
        top_b1,
        out_w,
    )
    gradients = gradients.reshape(devices, half_rows, 2, width)
    return lax.all_to_all(gradients, "dev", split_axis=0, concat_axis=0, tiled=True)


def solution(mesh):
    return jax.shard_map(
        local,
        mesh=mesh,
        in_specs=(
            P("dev", None, None),
            P(),
            P("dev", None),
            P("dev", None),
            P("dev", None),
            P("dev", None),
            P("dev"),
            P(),
            P(),
            P(),
            P(),
            P(),
            P(),
        ),
        out_specs=P(None, "role", "dev", None),
        check_vma=False,
    )
```

```python
import functools

import jax
import jax.numpy as jnp
from jax import lax
from jax.experimental import pallas as pl
from jax.experimental.pallas import tpu as pltpu
from jax.sharding import PartitionSpec as P

LANES = 128
CHUNK = 256
WIDEST = 272
NARROW = 192
FOLD = 512
GROUP = 4
PARTS = 8
MIB = 2**20


def pool_kernel(
    role_ref,
    tables,
    rows_hbm,
    bags_hbm,
    weights_hbm,
    pooled,
    folded,
    rows_ref,
    bags_ref,
    weights_ref,
    carried,
    picked,
    sems,
):
    role = role_ref[0]
    folds = tables.shape[1] // FOLD
    bag_count = pooled.shape[0]
    span = CHUNK * GROUP
    steps = rows_ref.shape[1] // span
    copies = [
        pltpu.make_async_copy(
            tables.at[role, pl.ds(fold * FOLD, FOLD)],
            folded.at[:, pl.ds(fold * LANES, LANES)],
            sems.at[fold],
        )
        for fold in range(folds)
    ]
    copies.append(pltpu.make_async_copy(rows_hbm, rows_ref, sems.at[folds]))
    later = [
        pltpu.make_async_copy(bags_hbm, bags_ref, sems.at[folds + 1]),
        pltpu.make_async_copy(weights_hbm, weights_ref, sems.at[folds + 2]),
    ]
    for copy in copies + later:
        copy.start()
    carried[...] = jnp.zeros_like(carried)
    for copy in copies:
        copy.wait()

    def own_row(ref, start, size):
        both = ref[:, pl.ds(pl.multiple_of(start, LANES), size)]
        if both.dtype != jnp.int32:
            both = both.astype(jnp.float32)
        return jnp.where(role == 0, both[0:1], both[1:2])

    def gather(step, slot):
        rows = own_row(rows_ref, step * span, span)
        index = jnp.concatenate(
            [
                jnp.broadcast_to(rows[:, at : at + LANES], (LANES, LANES)).T
                for at in range(0, span, LANES)
            ],
            axis=0,
        )
        within = (index & (FOLD - 1)).astype(jnp.int16)
        fold_of = index // FOLD
        lane = lax.broadcasted_iota(jnp.int32, (span, LANES), 1).astype(jnp.int16)
        hot = jnp.concatenate(
            [
                jnp.where(within == lane + jnp.int16(at), jnp.bfloat16(1), jnp.bfloat16(0))
                for at in range(0, FOLD, LANES)
            ],
            axis=1,
        )
        wide = jnp.dot(hot, folded[...], preferred_element_type=jnp.float32)
        found = wide[:, :LANES]
        for fold in range(1, folds):
            found = jnp.where(fold_of == fold, wide[:, fold * LANES : (fold + 1) * LANES], found)
        picked[slot] = found.astype(jnp.bfloat16)

    def scatter(step, slot, window, before):
        bags = own_row(bags_ref, step * span, span)
        weights = own_row(weights_ref, step * span, span)
        for inner in range(GROUP):
            at = inner * CHUNK
            base = jnp.minimum(bags[0, at] // 16 * 16, bag_count - window)
            block = (window, CHUNK)
            place = jnp.broadcast_to(bags[:, at : at + CHUNK] - base, block).astype(jnp.int16)
            scale = jnp.broadcast_to(weights[:, at : at + CHUNK], block).astype(jnp.bfloat16)
            sub = lax.broadcasted_iota(jnp.int32, block, 0).astype(jnp.int16)
            spread = jnp.where(sub == place, scale, jnp.bfloat16(0))
            sums = jnp.dot(
                spread, picked[slot, at : at + CHUNK, :], preferred_element_type=jnp.float32
            ) + carried[pl.ds(pl.multiple_of(base - before, 16), window), :]
            carried[:window, :] = sums
            pooled[pl.ds(pl.multiple_of(base, 16), window), :] = sums.astype(jnp.bfloat16)
            before = base
        return before

    gather(0, 0)
    for copy in later:
        copy.wait()

    def sweep(window):
        def pair(at, start):
            gather(2 * at + 1, 1)
            before = scatter(2 * at, 0, window, start)
            gather(2 * at + 2, 0)
            before = scatter(2 * at + 1, 1, window, before)
            return before

        start = lax.fori_loop(0, steps // 2 - 1, pair, jnp.int32(0), unroll=3)
        gather(steps - 1, 1)
        before = scatter(steps - 2, 0, window, start)
        scatter(steps - 1, 1, window, before)

    most = jnp.zeros((2, LANES), jnp.int32)
    for at in range(0, bags_ref.shape[1], CHUNK):
        ends = bags_ref[:, at + CHUNK - LANES : at + CHUNK]
        most = jnp.maximum(most, pltpu.roll(ends, 1, 1) - bags_ref[:, at : at + LANES])
    lane = lax.broadcasted_iota(jnp.int32, (2, LANES), 1)
    even = jnp.max(jnp.where(lane == 0, most, 0)) < NARROW - 16

    @pl.when(even)
    def _():
        sweep(NARROW)

    @pl.when(jnp.logical_not(even))
    def _():
        sweep(WIDEST)


def in_hbm(*values):
    return [pltpu.with_memory_space_constraint(value, pltpu.HBM) for value in values]


def pool_piece(role, table_rows, bag_rows, bag_of, bag_weight, bag_count):
    length, width = table_rows.shape[1:]
    anywhere = pl.BlockSpec(memory_space=pl.ANY)
    return pl.pallas_call(
        pool_kernel,
        in_specs=[pl.BlockSpec(memory_space=pltpu.SMEM)] + [anywhere] * 4,
        out_specs=pl.BlockSpec(memory_space=pltpu.VMEM),
        out_shape=jax.ShapeDtypeStruct((bag_count, width), jnp.bfloat16),
        scratch_shapes=[
            pltpu.VMEM((FOLD, length // FOLD * width), jnp.bfloat16),
            pltpu.VMEM(bag_rows.shape, jnp.int32),
            pltpu.VMEM(bag_of.shape, jnp.int32),
            pltpu.VMEM(bag_weight.shape, jnp.bfloat16),
            pltpu.VMEM((2 * WIDEST, width), jnp.float32),
            pltpu.VMEM((2, CHUNK * GROUP, width), jnp.bfloat16),
            pltpu.SemaphoreType.DMA((length // FOLD + 3,)),
        ],
        compiler_params=pltpu.CompilerParams(vmem_limit_bytes=40 * MIB),
    )(role, *in_hbm(table_rows, bag_rows, bag_of, bag_weight))


def against(left, right):
    return lax.dot_general(
        left, right, (((1,), (1,)), ((), ())), preferred_element_type=jnp.float32
    )


def dense_kernel(role_ref, cross_u, cross_v, top_w1, *refs):
    count = 7
    given, out_hbm, held = refs[:count], refs[count], refs[count + 1 : 2 * count + 1]
    features, cross, mixed, grad_mixed, grads, woven, leaving, sems, out_sem = refs[2 * count + 1 :]
    arrived, piece_table, dense_ref, label_ref, bias_ref, top_b1, out_w = held
    role = role_ref[0]
    pieces, rows, width = arrived.shape
    columns = features.shape[1]
    copies = [
        pltpu.make_async_copy(source, target, sems.at[at])
        for at, (source, target) in enumerate(zip(given[1:], held[1:]))
    ]
    parts = PARTS
    per_part = pieces // parts
    arrivals = [
        pltpu.make_async_copy(
            given[0].at[pl.ds(part * per_part, per_part)],
            arrived.at[pl.ds(part * per_part, per_part)],
            sems.at[count - 1 + part],
        )
        for part in range(parts)
    ]
    copies[0].start()
    for copy in arrivals + copies[1:]:
        copy.start()
    features[...] = jnp.zeros_like(features)
    copies[0].wait()
    for part in range(parts):
        arrivals[part].wait()

        @pl.loop(part * per_part, (part + 1) * per_part, unroll=4)
        def _(piece):
            place = pl.multiple_of((piece_table[0, piece] + 1) * width, width)
            features[:, pl.ds(place, width)] += arrived[piece].astype(jnp.float32)

    copies[1].wait()
    features[:, :width] = dense_ref[pl.ds(pl.multiple_of(role * rows, 16), rows), :].astype(
        jnp.float32
    )
    blocks = [(at, min(256, columns - at)) for at in range(0, columns, 256)]
    low_rank = jnp.dot(
        features[...].astype(jnp.bfloat16), cross_u[...], preferred_element_type=jnp.float32
    ).astype(jnp.bfloat16)
    copies[3].wait()
    for at, size in blocks:
        span = pl.ds(at, size)
        part_cross = (
            jnp.dot(low_rank, cross_v[:, span], preferred_element_type=jnp.float32)
            + bias_ref[span].reshape(1, size)
        )
        cross[:, span] = part_cross
        part_features = features[:, span]
        mixed[:, span] = (part_features * part_cross + part_features).astype(jnp.bfloat16)
    for at in (2, 4, 5):
        copies[at].wait()
    pre_act = jnp.dot(mixed[...], top_w1[...], preferred_element_type=jnp.float32) + top_b1[...].reshape(1, -1)
    out_weight = out_w[...].astype(jnp.float32).reshape(1, -1)
    sig_act = jax.nn.sigmoid(pre_act)
    logits = jnp.sum(pre_act * sig_act * out_weight, axis=1, keepdims=True)
    label_row = jnp.where(role == 0, label_ref[0:1, :], label_ref[1:2, :])
    label_column = jnp.broadcast_to(label_row, (rows, rows)).T[:, 0:1]
    grad_logit = jax.nn.sigmoid(logits) - label_column
    slope = sig_act * (1.0 + pre_act * (1.0 - sig_act))
    grad_act = (grad_logit * out_weight * slope).astype(jnp.bfloat16)
    for at, size in blocks:
        span = pl.ds(at, size)
        part_grad = against(grad_act, top_w1[span, :])
        grad_mixed[:, span] = part_grad
        mixed[:, span] = (part_grad * features[:, span]).astype(jnp.bfloat16)
    grad_low = against(mixed[...], cross_v[...]).astype(jnp.bfloat16)
    for at, size in blocks:
        span = pl.ds(at, size)
        total = grad_mixed[:, span] * (cross[:, span] + 1.0) + against(grad_low, cross_u[span, :])
        for inner in range(0, size, width):
            slot = (at + inner) // width - 1
            if slot >= 0:
                grads[slot] = total[:, inner : inner + width]

    @pl.loop(0, pieces // 2, unroll=4)
    def _(dest):
        slot = lax.rem(dest, woven.shape[0])
        for side in range(2):
            woven[slot, pl.ds(side, rows, stride=2), :] = grads[piece_table[0, 2 * dest + side]]
        leaving[dest] = woven[slot].astype(jnp.bfloat16)
        pltpu.make_async_copy(leaving.at[dest], out_hbm.at[dest], out_sem).start()

    pltpu.make_async_copy(leaving, out_hbm, out_sem).wait()


def dense_side(
    role, piece_table, arrived, dense_input, labels, cross_u, cross_v, cross_bias, top_w1, top_b1, out_w
):
    pieces, rows, width = arrived.shape
    columns = cross_bias.shape[0]
    anywhere = pl.BlockSpec(memory_space=pl.ANY)
    given = (
        arrived,
        piece_table.reshape(1, pieces),
        dense_input,
        labels.reshape(2, rows),
        cross_bias,
        top_b1,
        out_w,
    )
    held = [pltpu.VMEM(value.shape, value.dtype) for value in given]
    held[1] = pltpu.SMEM((1, pieces), jnp.int32)
    return pl.pallas_call(
        dense_kernel,
        in_specs=[pl.BlockSpec(memory_space=pltpu.SMEM)]
        + [pl.BlockSpec(memory_space=pltpu.VMEM)] * 3
        + [anywhere] * len(given),
        out_specs=anywhere,
        out_shape=pltpu.HBM((pieces // 2, 2 * rows, width), jnp.bfloat16),
        scratch_shapes=held
        + [
            pltpu.VMEM((rows, columns), jnp.float32),
            pltpu.VMEM((rows, columns), jnp.float32),
            pltpu.VMEM((rows, columns), jnp.bfloat16),
            pltpu.VMEM((rows, columns), jnp.float32),
            pltpu.VMEM((columns // width - 1, rows, width), jnp.float32),
            pltpu.VMEM((4, 2 * rows, width), jnp.float32),
            pltpu.VMEM((pieces // 2, 2 * rows, width), jnp.bfloat16),
            pltpu.SemaphoreType.DMA((len(given) - 1 + PARTS,)),
            pltpu.SemaphoreType.DMA,
        ],
        compiler_params=pltpu.CompilerParams(vmem_limit_bytes=40 * MIB),
    )(role, cross_u, cross_v, top_w1, *in_hbm(*given))


def local(
    table_rows,
    piece_table,
    bag_rows,
    bag_of,
    bag_weight,
    dense_input,
    labels,
    cross_u,
    cross_v,
    cross_bias,
    top_w1,
    top_b1,
    out_w,
):
    devices = lax.axis_size("dev")
    role = lax.axis_index("role").reshape(1)
    half_rows = dense_input.shape[0] // 2
    width = dense_input.shape[1]
    pooled = pool_piece(
        role, table_rows, bag_rows, bag_of, bag_weight, devices * dense_input.shape[0]
    )
    arrived = lax.all_to_all(
        pooled.reshape(2 * devices, half_rows, width),
        ("dev", "role"),
        split_axis=0,
        concat_axis=0,
        tiled=True,
    )
    gradients = dense_side(
        role,
        piece_table,
        arrived,
        dense_input,
        labels,
        cross_u,
        cross_v,
        cross_bias,
        top_w1,
        top_b1,
        out_w,
    )
    gradients = gradients.reshape(devices, half_rows, 2, width)
    return lax.all_to_all(gradients, "dev", split_axis=0, concat_axis=0, tiled=True)


def solution(mesh):
    return jax.shard_map(
        local,
        mesh=mesh,
        in_specs=(
            P("dev", None, None),
            P(),
            P("dev", None),
            P("dev", None),
            P("dev", None),
            P("dev", None),
            P("dev"),
            P(),
            P(),
            P(),
            P(),
            P(),
            P(),
        ),
        out_specs=P(None, "role", "dev", None),
        check_vma=False,
    )
```

```python
import functools

import jax
import jax.numpy as jnp
from jax import lax
from jax.experimental import pallas as pl
from jax.experimental.pallas import tpu as pltpu
from jax.sharding import PartitionSpec as P

LANES = 128
CHUNK = 256
WIDEST = 272
NARROW = 192
FOLD = 512
GROUP = 4
PARTS = 8
MIB = 2**20


def pool_kernel(
    role_ref,
    tables,
    rows_hbm,
    bags_hbm,
    weights_hbm,
    pooled,
    folded,
    rows_ref,
    bags_ref,
    weights_ref,
    carried,
    picked,
    sems,
):
    role = role_ref[0]
    folds = tables.shape[1] // FOLD
    bag_count = pooled.shape[0]
    span = CHUNK * GROUP
    steps = rows_ref.shape[1] // span
    copies = [
        pltpu.make_async_copy(
            tables.at[role, pl.ds(fold * FOLD, FOLD)],
            folded.at[:, pl.ds(fold * LANES, LANES)],
            sems.at[fold],
        )
        for fold in range(folds)
    ]
    copies.append(pltpu.make_async_copy(rows_hbm, rows_ref, sems.at[folds]))
    later = [
        pltpu.make_async_copy(bags_hbm, bags_ref, sems.at[folds + 1]),
        pltpu.make_async_copy(weights_hbm, weights_ref, sems.at[folds + 2]),
    ]
    for copy in copies + later:
        copy.start()
    carried[...] = jnp.zeros_like(carried)
    for copy in copies:
        copy.wait()

    def own_row(ref, start, size):
        both = ref[:, pl.ds(pl.multiple_of(start, LANES), size)]
        if both.dtype != jnp.int32:
            both = both.astype(jnp.float32)
        return jnp.where(role == 0, both[0:1], both[1:2])

    def gather(step, slot):
        rows = own_row(rows_ref, step * span, span)
        index = jnp.concatenate(
            [
                jnp.broadcast_to(rows[:, at : at + LANES], (LANES, LANES)).T
                for at in range(0, span, LANES)
            ],
            axis=0,
        )
        within = (index & (FOLD - 1)).astype(jnp.int16)
        fold_of = index // FOLD
        lane = lax.broadcasted_iota(jnp.int32, (span, LANES), 1).astype(jnp.int16)
        hot = jnp.concatenate(
            [
                jnp.where(within == lane + jnp.int16(at), jnp.bfloat16(1), jnp.bfloat16(0))
                for at in range(0, FOLD, LANES)
            ],
            axis=1,
        )
        wide = jnp.dot(hot, folded[...], preferred_element_type=jnp.float32)
        found = wide[:, :LANES]
        for fold in range(1, folds):
            found = jnp.where(fold_of == fold, wide[:, fold * LANES : (fold + 1) * LANES], found)
        picked[slot] = found.astype(jnp.bfloat16)

    def scatter(step, slot, window, before):
        bags = own_row(bags_ref, step * span, span)
        weights = own_row(weights_ref, step * span, span)
        for inner in range(GROUP):
            at = inner * CHUNK
            base = jnp.minimum(bags[0, at] // 16 * 16, bag_count - window)
            block = (window, CHUNK)
            place = jnp.broadcast_to(bags[:, at : at + CHUNK] - base, block).astype(jnp.int16)
            scale = jnp.broadcast_to(weights[:, at : at + CHUNK], block).astype(jnp.bfloat16)
            sub = lax.broadcasted_iota(jnp.int32, block, 0).astype(jnp.int16)
            spread = jnp.where(sub == place, scale, jnp.bfloat16(0))
            sums = jnp.dot(
                spread, picked[slot, at : at + CHUNK, :], preferred_element_type=jnp.float32
            ) + carried[pl.ds(pl.multiple_of(base - before, 16), window), :]
            carried[:window, :] = sums
            pooled[pl.ds(pl.multiple_of(base, 16), window), :] = sums.astype(jnp.bfloat16)
            before = base
        return before

    gather(0, 0)
    for copy in later:
        copy.wait()

    def sweep(window):
        def pair(at, start):
            gather(2 * at + 1, 1)
            before = scatter(2 * at, 0, window, start)
            gather(2 * at + 2, 0)
            before = scatter(2 * at + 1, 1, window, before)
            return before

        start = lax.fori_loop(0, steps // 2 - 1, pair, jnp.int32(0), unroll=3)
        gather(steps - 1, 1)
        before = scatter(steps - 2, 0, window, start)
        scatter(steps - 1, 1, window, before)

    most = jnp.zeros((2, LANES), jnp.int32)
    for at in range(0, bags_ref.shape[1], CHUNK):
        ends = bags_ref[:, at + CHUNK - LANES : at + CHUNK]
        most = jnp.maximum(most, pltpu.roll(ends, 1, 1) - bags_ref[:, at : at + LANES])
    lane = lax.broadcasted_iota(jnp.int32, (2, LANES), 1)
    even = jnp.max(jnp.where(lane == 0, most, 0)) < NARROW - 16

    @pl.when(even)
    def _():
        sweep(NARROW)

    @pl.when(jnp.logical_not(even))
    def _():
        sweep(WIDEST)


def in_hbm(*values):
    return [pltpu.with_memory_space_constraint(value, pltpu.HBM) for value in values]


def pool_piece(role, table_rows, bag_rows, bag_of, bag_weight, bag_count):
    length, width = table_rows.shape[1:]
    anywhere = pl.BlockSpec(memory_space=pl.ANY)
    return pl.pallas_call(
        pool_kernel,
        in_specs=[pl.BlockSpec(memory_space=pltpu.SMEM)] + [anywhere] * 4,
        out_specs=pl.BlockSpec(memory_space=pltpu.VMEM),
        out_shape=jax.ShapeDtypeStruct((bag_count, width), jnp.bfloat16),
        scratch_shapes=[
            pltpu.VMEM((FOLD, length // FOLD * width), jnp.bfloat16),
            pltpu.VMEM(bag_rows.shape, jnp.int32),
            pltpu.VMEM(bag_of.shape, jnp.int32),
            pltpu.VMEM(bag_weight.shape, jnp.bfloat16),
            pltpu.VMEM((2 * WIDEST, width), jnp.float32),
            pltpu.VMEM((2, CHUNK * GROUP, width), jnp.bfloat16),
            pltpu.SemaphoreType.DMA((length // FOLD + 3,)),
        ],
        compiler_params=pltpu.CompilerParams(vmem_limit_bytes=40 * MIB),
    )(role, *in_hbm(table_rows, bag_rows, bag_of, bag_weight))


def against(left, right):
    return lax.dot_general(
        left, right, (((1,), (1,)), ((), ())), preferred_element_type=jnp.float32
    )


def dense_kernel(role_ref, cross_u, cross_v, top_w1, *refs):
    count = 7
    given, out_hbm, held = refs[:count], refs[count], refs[count + 1 : 2 * count + 1]
    features, cross, mixed, grad_mixed, grads, woven, leaving, sems, out_sem = refs[2 * count + 1 :]
    arrived, piece_table, dense_ref, label_ref, bias_ref, top_b1, out_w = held
    role = role_ref[0]
    pieces, rows, width = arrived.shape
    columns = features.shape[1]
    copies = [
        pltpu.make_async_copy(source, target, sems.at[at])
        for at, (source, target) in enumerate(zip(given[1:], held[1:]))
    ]
    parts = PARTS
    per_part = pieces // parts
    arrivals = [
        pltpu.make_async_copy(
            given[0].at[pl.ds(part * per_part, per_part)],
            arrived.at[pl.ds(part * per_part, per_part)],
            sems.at[count - 1 + part],
        )
        for part in range(parts)
    ]
    copies[0].start()
    for copy in arrivals + copies[1:]:
        copy.start()
    features[...] = jnp.zeros_like(features)
    copies[0].wait()
    for part in range(parts):
        arrivals[part].wait()

        @pl.loop(part * per_part, (part + 1) * per_part, unroll=4)
        def _(piece):
            place = pl.multiple_of((piece_table[0, piece] + 1) * width, width)
            features[:, pl.ds(place, width)] += arrived[piece].astype(jnp.float32)

    copies[1].wait()
    features[:, :width] = dense_ref[pl.ds(pl.multiple_of(role * rows, 16), rows), :].astype(
        jnp.float32
    )
    blocks = [(at, min(256, columns - at)) for at in range(0, columns, 256)]
    low_rank = jnp.dot(
        features[...].astype(jnp.bfloat16), cross_u[...], preferred_element_type=jnp.float32
    ).astype(jnp.bfloat16)
    copies[3].wait()
    for at, size in blocks:
        span = pl.ds(at, size)
        part_cross = (
            jnp.dot(low_rank, cross_v[:, span], preferred_element_type=jnp.float32)
            + bias_ref[span].reshape(1, size)
        )
        cross[:, span] = part_cross
        part_features = features[:, span]
        mixed[:, span] = (part_features * part_cross + part_features).astype(jnp.bfloat16)
    for at in (2, 4, 5):
        copies[at].wait()
    pre_act = jnp.dot(mixed[...], top_w1[...], preferred_element_type=jnp.float32) + top_b1[...].reshape(1, -1)
    out_weight = out_w[...].astype(jnp.float32).reshape(1, -1)
    sig_act = jax.nn.sigmoid(pre_act)
    logits = jnp.sum(pre_act * sig_act * out_weight, axis=1, keepdims=True)
    label_row = jnp.where(role == 0, label_ref[0:1, :], label_ref[1:2, :])
    label_column = jnp.broadcast_to(label_row, (rows, rows)).T[:, 0:1]
    grad_logit = jax.nn.sigmoid(logits) - label_column
    slope = sig_act * (1.0 + pre_act * (1.0 - sig_act))
    grad_act = (grad_logit * out_weight * slope).astype(jnp.bfloat16)
    for at, size in blocks:
        span = pl.ds(at, size)
        part_grad = against(grad_act, top_w1[span, :])
        grad_mixed[:, span] = part_grad
        mixed[:, span] = (part_grad * features[:, span]).astype(jnp.bfloat16)
    grad_low = against(mixed[...], cross_v[...]).astype(jnp.bfloat16)
    for at, size in blocks:
        span = pl.ds(at, size)
        total = grad_mixed[:, span] * (cross[:, span] + 1.0) + against(grad_low, cross_u[span, :])
        for inner in range(0, size, width):
            slot = (at + inner) // width - 1
            if slot >= 0:
                grads[slot] = total[:, inner : inner + width]

    slots = woven.shape[0]

    @pl.loop(0, pieces // 2, step=slots)
    def _(first):
        for slot in range(slots):
            for side in range(2):
                piece = 2 * (first + slot) + side
                woven[slot, pl.ds(side, rows, stride=2), :] = grads[piece_table[0, piece]]
        for slot in range(slots):
            leaving[first + slot] = woven[slot].astype(jnp.bfloat16)
        group = pl.ds(first, slots)
        pltpu.make_async_copy(leaving.at[group], out_hbm.at[group], out_sem).start()

    pltpu.make_async_copy(leaving, out_hbm, out_sem).wait()


def dense_side(
    role, piece_table, arrived, dense_input, labels, cross_u, cross_v, cross_bias, top_w1, top_b1, out_w
):
    pieces, rows, width = arrived.shape
    columns = cross_bias.shape[0]
    anywhere = pl.BlockSpec(memory_space=pl.ANY)
    given = (
        arrived,
        piece_table.reshape(1, pieces),
        dense_input,
        labels.reshape(2, rows),
        cross_bias,
        top_b1,
        out_w,
    )
    held = [pltpu.VMEM(value.shape, value.dtype) for value in given]
    held[1] = pltpu.SMEM((1, pieces), jnp.int32)
    return pl.pallas_call(
        dense_kernel,
        in_specs=[pl.BlockSpec(memory_space=pltpu.SMEM)]
        + [pl.BlockSpec(memory_space=pltpu.VMEM)] * 3
        + [anywhere] * len(given),
        out_specs=anywhere,
        out_shape=pltpu.HBM((pieces // 2, 2 * rows, width), jnp.bfloat16),
        scratch_shapes=held
        + [
            pltpu.VMEM((rows, columns), jnp.float32),
            pltpu.VMEM((rows, columns), jnp.float32),
            pltpu.VMEM((rows, columns), jnp.bfloat16),
            pltpu.VMEM((rows, columns), jnp.float32),
            pltpu.VMEM((columns // width - 1, rows, width), jnp.float32),
            pltpu.VMEM((8, 2 * rows, width), jnp.float32),
            pltpu.VMEM((pieces // 2, 2 * rows, width), jnp.bfloat16),
            pltpu.SemaphoreType.DMA((len(given) - 1 + PARTS,)),
            pltpu.SemaphoreType.DMA,
        ],
        compiler_params=pltpu.CompilerParams(vmem_limit_bytes=40 * MIB),
    )(role, cross_u, cross_v, top_w1, *in_hbm(*given))


def local(
    table_rows,
    piece_table,
    bag_rows,
    bag_of,
    bag_weight,
    dense_input,
    labels,
    cross_u,
    cross_v,
    cross_bias,
    top_w1,
    top_b1,
    out_w,
):
    devices = lax.axis_size("dev")
    role = lax.axis_index("role").reshape(1)
    half_rows = dense_input.shape[0] // 2
    width = dense_input.shape[1]
    pooled = pool_piece(
        role, table_rows, bag_rows, bag_of, bag_weight, devices * dense_input.shape[0]
    )
    arrived = lax.all_to_all(
        pooled.reshape(2 * devices, half_rows, width),
        ("dev", "role"),
        split_axis=0,
        concat_axis=0,
        tiled=True,
    )
    gradients = dense_side(
        role,
        piece_table,
        arrived,
        dense_input,
        labels,
        cross_u,
        cross_v,
        cross_bias,
        top_w1,
        top_b1,
        out_w,
    )
    gradients = gradients.reshape(devices, half_rows, 2, width)
    return lax.all_to_all(gradients, "dev", split_axis=0, concat_axis=0, tiled=True)


def solution(mesh):
    return jax.shard_map(
        local,
        mesh=mesh,
        in_specs=(
            P("dev", None, None),
            P(),
            P("dev", None),
            P("dev", None),
            P("dev", None),
            P("dev", None),
            P("dev"),
            P(),
            P(),
            P(),
            P(),
            P(),
            P(),
        ),
        out_specs=P(None, "role", "dev", None),
        check_vma=False,
    )
```
